32 devices in a mesh: patch: 2 (over y), visit: 4 (over z), tile: 4 (over x, core).
Axes of the slice: x: 2, y: 2, z: 4, core: 2. Of those that a mesh axis runs over, the one named last changes fastest.
Arguments:
- exposure: float32 [16, 256, 4096], P('visit', ('patch', 'tile')), parts along dimension 1, may hold values from -12 to 12
- variance: float32 [16, 256, 4096], P('visit', ('patch', 'tile')), parts along dimension 1, may hold values from 0.25 to 4
- usable: int32 [16, 256, 4096], P('visit', ('patch', 'tile')), parts along dimension 1, may hold values from 0 to 1, as said below
- basis_width: float32 [32, 3], P(('patch', 'visit')), parts along dimension 0, may hold values from 0.8 to 3.5
- spatial_coef: float32 [32, 3, 6], P(('patch', 'visit')), parts along dimension 0, may hold values from -0.6 to 1.4
Outputs:
- coadd: float32 [256, 4096], P(('patch', 'tile')), parts along dimension 0
The draws below stay inside these ranges and needn't reach their ends.
There are 2 independent parts, one for each index of `patch`. The reference program is written for one: setup_inputs(seed, part) draws one part's arguments, and reference() takes and returns one part's arrays. A program takes and returns all parts, laid end to end along the dimension named above; each array names one. Nothing has to cross between parts.
Inputs may be any that keep to these rules, and one draw needn't show every extreme that they name: 1 marks a usable sample; at every pixel at least 5 of the 16 visits are usable.
All inputs are finite; a program needn't handle non-finite values.
Results may differ from the reference program's by a relative error of at most 0.0003.
Values sent between devices are 32-bit elements; how exact they have to be, the bound alone decides.
A program may use at most 128 MiB of HBM per device.

```python
import math
import jax
import jax.numpy as jnp
from jax import lax

W = 4096
KHALF = 15
BASES = 3
TERMS = 6
VISITS = 16
ROWS = 128


def draw_exposure(key, part):
    base_key = jax.random.fold_in(key, 11)
    sky_key, noise_key, hit_key = jax.random.split(base_key, 3)
    sky_field = jax.random.normal(sky_key, (ROWS, W), jnp.float32)
    hits = (jax.random.randint(hit_key, (VISITS, ROWS, W), 0, 64) == 0).astype(jnp.float32)
    noise = jax.random.normal(noise_key, (VISITS, ROWS, W), jnp.float32)
    sky_field = 1.5 * sky_field
    return jnp.clip(sky_field[None] + noise + 6.0 * hits, -12.0, 12.0)


def draw_usable(key, part):
    base_key = jax.random.fold_in(key, 23)
    rough_key, offset_key = jax.random.split(base_key, 2)
    rough = jax.random.randint(rough_key, (VISITS, ROWS, W), 0, 8) != 0
    offset = jax.random.randint(offset_key, (ROWS, W), 0, VISITS)
    visit_ids = jnp.arange(VISITS).astype(jnp.int32)[:, None, None]
    kept = (visit_ids - offset[None]) % VISITS < 5
    return jnp.logical_or(rough, kept).astype(jnp.int32)


def draw_spatial_coef(key, part):
    base_key = jax.random.fold_in(key, 37)
    rest_key, main_key = jax.random.split(base_key, 2)
    rest = jnp.clip(0.15 * jax.random.normal(rest_key, (VISITS, BASES, TERMS), jnp.float32), -0.6, 0.6)
    main = jnp.clip(1.0 + 0.1 * jax.random.normal(main_key, (VISITS,), jnp.float32), 0.6, 1.4)
    return rest.at[:, 0, 0].set(main)


def block_scale(key, dims, pieces, low, high):
    factor_of, own = 1.0, jax.random.fold_in(key, 6)
    for position, blocks in pieces:
        steps = jnp.exp(jax.random.uniform(jax.random.fold_in(own, position), (blocks,), jnp.float32, low / len(pieces), high / len(pieces)))
        factor_of = factor_of * jnp.repeat(steps, dims[position] // blocks).reshape([-1 if axis == position else 1 for axis in range(len(dims))])
    return factor_of


def setup_inputs(seed: int = 0, part: int = 0) -> dict:
    splits = jax.random.split(jax.random.key(seed), 6)
    part_splits = jax.random.split(jax.random.fold_in(splits[5], part), 6)
    exposure = draw_exposure(jax.random.fold_in(jax.random.fold_in(splits[5], part), 71), part)
    variance = jnp.clip(jnp.exp(math.log(4.0) - 2.7725887 * jax.random.uniform(part_splits[1], (VISITS, ROWS, W), jnp.float32) ** block_scale(part_splits[1], (VISITS, ROWS, W), ((0, 4), (1, 4)), -0.2, 0.2)), 0.25, 4.0)
    usable = draw_usable(jax.random.fold_in(jax.random.fold_in(splits[5], part), 71), part)
    basis_width = jnp.clip(jnp.exp(math.log(3.5) - 1.4759065 * jax.random.uniform(part_splits[3], (VISITS, BASES), jnp.float32) ** block_scale(part_splits[3], (VISITS, BASES), ((0, 4),), -0.2, 0.2)), 0.8, 3.5)
    spatial_coef = draw_spatial_coef(jax.random.fold_in(jax.random.fold_in(splits[5], part), 71), part)
    return {"exposure": exposure, "variance": variance, "usable": usable, "basis_width": basis_width, "spatial_coef": spatial_coef}


def basis_profile(offsets, width, basis_id):
    profile = jnp.exp(-offsets * offsets / (2.0 * width * width))
    if basis_id > 0:
        profile = profile * (offsets / width) ** (2 * basis_id)
    return profile


def reference(exposure, variance, usable, basis_width, spatial_coef):
    offsets = jnp.arange(-KHALF, KHALF + 1).astype(jnp.float32)
    row_pos = 2.0 * jnp.arange(ROWS).astype(jnp.float32) / (ROWS - 1) - 1.0
    col_pos = 2.0 * jnp.arange(W).astype(jnp.float32) / (W - 1) - 1.0
    ycoord = jnp.broadcast_to(row_pos[:, None], (ROWS, W))
    xcoord = jnp.broadcast_to(col_pos[None, :], (ROWS, W))
    poly_terms = [jnp.ones((ROWS, W), jnp.float32), xcoord, ycoord, xcoord * xcoord, xcoord * ycoord, ycoord * ycoord]

    def one_visit(inputs):
        image, widths, coefs = inputs
        padded = jnp.pad(image, KHALF)
        matched = jnp.zeros((ROWS, W), jnp.float32)
        for basis_id in range(BASES):
            profile = basis_profile(offsets, widths[basis_id], basis_id)
            profile = profile / jnp.sum(profile)
            vertical = jnp.zeros((ROWS, W + 2 * KHALF), jnp.float32)
            for shift_id in range(2 * KHALF + 1):
                vertical = vertical + profile[shift_id] * padded[shift_id:shift_id + ROWS, :]
            smoothed = jnp.zeros((ROWS, W), jnp.float32)
            for shift_id in range(2 * KHALF + 1):
                smoothed = smoothed + profile[shift_id] * vertical[:, shift_id:shift_id + W]
            factor = jnp.zeros((ROWS, W), jnp.float32)
            for term_id in range(TERMS):
                factor = factor + coefs[basis_id, term_id] * poly_terms[term_id]
            matched = matched + factor * smoothed
        return matched

    matched = lax.map(one_visit, (exposure, basis_width, spatial_coef))
    valid = usable > 0
    big_value = 1e30
    lower = jnp.sort(jnp.where(valid, matched, big_value), axis=0)[2]
    upper = jnp.sort(jnp.where(valid, matched, -big_value), axis=0)[-3]
    weight = jnp.where(valid, 1.0 / variance, 0.0)
    numer = jnp.sum(weight * jnp.clip(matched, lower, upper), axis=0)
    denom = jnp.sum(weight, axis=0)
    return numer / denom
```

```python
import functools

import jax
import jax.numpy as jnp
from jax import lax
from jax.experimental import pallas as pl
from jax.experimental.pallas import tpu as pltpu
from jax.sharding import PartitionSpec as P

KHALF = 15
BASES = 3
TERMS = 6
HALO = 16
BLOCK = 256
SIDE = 128
SCALARS = 2 + TERMS
MESH = pl.DeviceIdType.MESH

big_value = 1e30


def band(offsets, narrow, norm, basis_id):
    square = (offsets * offsets).astype(jnp.float32)
    profile = jnp.exp(-square * narrow) * norm
    for _ in range(basis_id):
        profile = profile * (square * (2.0 * narrow))
    return jnp.where(jnp.abs(offsets) <= KHALF, profile, 0.0)


def split(values):
    high = values.astype(jnp.bfloat16)
    low = (values - high.astype(jnp.float32)).astype(jnp.bfloat16)
    return high, low


def dot(a, b):
    return jnp.dot(a, b, preferred_element_type=jnp.float32)


def kernel(
    tiles, owners,
    scal_ref, expo_ref, var_ref, use_ref, out_ref,
    halo, w_own, m_own, w_got, m_got, vert_hi, vert_lo, total, result,
    halo_send, halo_got, w_send, w_recv, m_send, m_recv, r_send, r_recv,
):
    visits, rows, cols = expo_ref.shape
    blocks = cols // BLOCK
    mine_blocks = blocks // owners
    share = mine_blocks * rows
    me = lax.axis_index("visit")
    tile = lax.axis_index("tile")
    has_up = tile > 0
    has_down = tile < tiles - 1
    peers = [lax.rem(me + d, owners) for d in range(1, owners)]

    barrier = pltpu.get_barrier_semaphore()
    for peer in peers:
        pl.semaphore_signal(barrier, inc=1, device_id={"visit": peer}, device_id_type=MESH)

    @pl.when(has_up)
    def _():
        pl.semaphore_signal(barrier, inc=1, device_id={"tile": tile - 1}, device_id_type=MESH)

    @pl.when(has_down)
    def _():
        pl.semaphore_signal(barrier, inc=1, device_id={"tile": tile + 1}, device_id_type=MESH)

    beside = has_up.astype(jnp.int32) + has_down.astype(jnp.int32)
    pl.semaphore_wait(barrier, owners - 1 + beside)

    def halo_copy(side, v):
        start = rows - HALO if side == 0 else 0
        return pltpu.make_async_remote_copy(
            src_ref=expo_ref.at[v, pl.ds(start, HALO), :],
            dst_ref=halo.at[side, v],
            send_sem=halo_send.at[side, v],
            recv_sem=halo_got.at[side, v],
            device_id={"tile": tile + 1 if side == 0 else tile - 1},
            device_id_type=MESH,
        )

    @pl.when(has_down)
    def _():
        for v in range(visits):
            halo_copy(0, v).start()

    @pl.when(has_up)
    def _():
        for v in range(visits):
            halo_copy(1, v).start()

    @pl.when(jnp.logical_not(has_up))
    def _():
        halo[0] = jnp.zeros(halo.shape[1:], jnp.float32)

    @pl.when(jnp.logical_not(has_down))
    def _():
        halo[1] = jnp.zeros(halo.shape[1:], jnp.float32)

    def w_copy(peer, k):
        return pltpu.make_async_remote_copy(
            src_ref=w_own.at[peer], dst_ref=w_got.at[me],
            send_sem=w_send.at[k], recv_sem=w_recv.at[me],
            device_id={"visit": peer}, device_id_type=MESH,
        )

    def m_copy(peer, k, v):
        return pltpu.make_async_remote_copy(
            src_ref=m_own.at[peer, v], dst_ref=m_got.at[me, v],
            send_sem=m_send.at[k, v], recv_sem=m_recv.at[me, v],
            device_id={"visit": peer}, device_id_type=MESH,
        )

    def r_copy(peer, k):
        return pltpu.make_async_remote_copy(
            src_ref=result.at[me], dst_ref=result.at[me],
            send_sem=r_send.at[k], recv_sem=r_recv.at[me],
            device_id={"visit": peer}, device_id_type=MESH,
        )

    def weights_for(owner):
        def step(v, carry):
            for j in range(mine_blocks):
                first = pl.multiple_of((owner * mine_blocks + j) * BLOCK, BLOCK)
                there = pl.ds(first, BLOCK)
                w_own[owner, v, pl.ds(j * rows, rows), :] = jnp.where(
                    use_ref[v, :, there] > 0, 1.0 / var_ref[v, :, there], 0.0
                )
            return carry

        lax.fori_loop(0, visits, step, 0)

    for k, peer in enumerate(peers):
        weights_for(peer)
        w_copy(peer, k).start()
    weights_for(me)

    wide = cols + 2 * SIDE
    for ref in (vert_hi, vert_lo):
        ref[:, pl.ds(0, SIDE)] = jnp.zeros((BASES * rows, SIDE), jnp.bfloat16)
        ref[:, pl.ds(wide - SIDE, SIDE)] = jnp.zeros((BASES * rows, SIDE), jnp.bfloat16)

    reach = rows + 2 * HALO
    depth = BLOCK + 2 * SIDE
    stacked = blocks * rows

    def visit_step(v, carry):
        @pl.when(has_up)
        def _():
            halo_copy(0, v).wait_recv()

        @pl.when(has_down)
        def _():
            halo_copy(1, v).wait_recv()

        out_row = lax.broadcasted_iota(jnp.int32, (rows, 3 * reach), 0)
        in_row = lax.broadcasted_iota(jnp.int32, (rows, 3 * reach), 1)
        third = in_row >= 2 * reach
        in_row = jnp.where(third, in_row - 2 * reach, jnp.where(in_row >= reach, in_row - reach, in_row))
        pieces = []
        for b in range(BASES):
            mat = band(in_row - HALO - out_row, scal_ref[v, b * SCALARS], scal_ref[v, b * SCALARS + 1], b)
            high = mat.astype(jnp.bfloat16).astype(jnp.float32)
            pieces.append(jnp.where(third, mat - high, high))
        down = jnp.concatenate(pieces, axis=0).astype(jnp.bfloat16)

        def column_step(n, inner):
            there = pl.ds(pl.multiple_of(n * 2 * BLOCK, 2 * BLOCK), 2 * BLOCK)
            image = jnp.concatenate([halo[0, v, :, there], expo_ref[v, :, there], halo[1, v, :, there]], axis=0)
            high, low = split(image)
            vert = dot(down, jnp.concatenate([high, low, high], axis=0))
            high, low = split(vert)
            here = pl.ds(pl.multiple_of(n * 2 * BLOCK + SIDE, SIDE), 2 * BLOCK)
            vert_hi[:, here] = high
            vert_lo[:, here] = low
            return inner

        lax.fori_loop(0, blocks // 2, column_step, 0)

        in_col = lax.broadcasted_iota(jnp.int32, (depth, BLOCK), 0)
        out_col = lax.broadcasted_iota(jnp.int32, (depth, BLOCK), 1)
        for b in range(BASES):
            narrow, norm = scal_ref[v, b * SCALARS], scal_ref[v, b * SCALARS + 1]
            across_hi, across_lo = split(band(in_col - SIDE - out_col, narrow, norm, b))
            c = [scal_ref[v, b * SCALARS + 2 + k] for k in range(TERMS)]
            for d in range(owners):
                left = [
                    jnp.concatenate(
                        [
                            ref[pl.ds(b * rows, rows), pl.ds((d * mine_blocks + j) * BLOCK, depth)]
                            for j in range(mine_blocks)
                        ],
                        axis=0,
                    )
                    for ref in (vert_hi, vert_lo)
                ]
                smooth = dot(left[0], across_hi) + dot(left[1], across_hi) + dot(left[0], across_lo)
                row = lax.broadcasted_iota(jnp.int32, (share, BLOCK), 0)
                col = lax.broadcasted_iota(jnp.int32, (share, BLOCK), 1)
                col = col + (d * mine_blocks + row // rows) * BLOCK
                row = row % rows + tile * rows
                y = row.astype(jnp.float32) * (2.0 / (tiles * rows - 1)) - 1.0
                x = col.astype(jnp.float32) * (2.0 / (cols - 1)) - 1.0
                factor = (c[0] + y * (c[2] + y * c[5])) + x * (c[1] + y * c[4] + x * c[3])
                term = factor * smooth
                here = pl.ds(d * share, share)
                if b == 0:
                    total[here, :] = term
                elif b < BASES - 1:
                    total[here, :] += term
                else:
                    m_own[d, v] = total[here, :] + term
        for k, peer in enumerate(peers):
            m_copy(peer, k, v).start()
        return carry

    lax.fori_loop(0, visits, visit_step, 0)

    def got_w(s):
        return pltpu.make_async_remote_copy(
            src_ref=w_own.at[s], dst_ref=w_got.at[s], send_sem=w_send.at[0], recv_sem=w_recv.at[s],
            device_id={"visit": s}, device_id_type=MESH,
        )

    def got_m(s, v):
        return pltpu.make_async_remote_copy(
            src_ref=m_own.at[s, v], dst_ref=m_got.at[s, v], send_sem=m_send.at[0, v], recv_sem=m_recv.at[s, v],
            device_id={"visit": s}, device_id_type=MESH,
        )

    def got_r(s):
        return pltpu.make_async_remote_copy(
            src_ref=result.at[s], dst_ref=result.at[s], send_sem=r_send.at[0], recv_sem=r_recv.at[s],
            device_id={"visit": s}, device_id_type=MESH,
        )

    for peer in peers:
        got_w(peer).wait_recv()
        for v in range(visits):
            got_m(peer, v).wait_recv()

    sources = [(m_own, w_own, me)] + [(m_got, w_got, peer) for peer in peers]
    strip = 16

    def strip_step(i, carry):
        here = pl.ds(pl.multiple_of(i * strip, strip), strip)
        full = jnp.full((strip, BLOCK), big_value, jnp.float32)
        l1 = l2 = l3 = full
        h1 = h2 = h3 = -full
        for m_ref, w_ref, s in sources:
            for v in range(visits):
                m = m_ref[s, v, here, :]
                valid = w_ref[s, v, here, :] > 0.0
                low = jnp.where(valid, m, big_value)
                high = jnp.where(valid, m, -big_value)
                l3 = jnp.minimum(l3, jnp.maximum(l2, low))
                l2 = jnp.minimum(l2, jnp.maximum(l1, low))
                l1 = jnp.minimum(l1, low)
                h3 = jnp.maximum(h3, jnp.minimum(h2, high))
                h2 = jnp.maximum(h2, jnp.minimum(h1, high))
                h1 = jnp.maximum(h1, high)
        numer = jnp.zeros((strip, BLOCK), jnp.float32)
        denom = numer
        for m_ref, w_ref, s in sources:
            for v in range(visits):
                w = w_ref[s, v, here, :]
                m = jnp.minimum(jnp.maximum(m_ref[s, v, here, :], l3), h3)
                numer = numer + w * m
                denom = denom + w
        result[me, here, :] = numer / denom
        return carry

    lax.fori_loop(0, share // strip, strip_step, 0)
    for k, peer in enumerate(peers):
        r_copy(peer, k).start()
    for peer in peers:
        got_r(peer).wait_recv()
    for s in range(owners):
        for j in range(mine_blocks):
            out_ref[:, pl.ds((s * mine_blocks + j) * BLOCK, BLOCK)] = result[s, pl.ds(j * rows, rows), :]

    for k, peer in enumerate(peers):
        w_copy(peer, k).wait_send()
        for v in range(visits):
            m_copy(peer, k, v).wait_send()
        r_copy(peer, k).wait_send()

    @pl.when(has_down)
    def _():
        for v in range(visits):
            halo_copy(0, v).wait_send()

    @pl.when(has_up)
    def _():
        for v in range(visits):
            halo_copy(1, v).wait_send()


def per_device(exposure, variance, usable, basis_width, spatial_coef):
    visits, rows, cols = exposure.shape
    tiles, owners = lax.axis_size("tile"), lax.axis_size("visit")
    share = cols // BLOCK // owners * rows
    narrow = 0.5 / (basis_width * basis_width)
    offsets = jnp.arange(-KHALF, KHALF + 1).astype(jnp.float32)
    square = (offsets * offsets)[None, None, :]
    powers = [jnp.ones_like(square), square, square * square]
    raw = jnp.exp(-square * narrow[:, :, None]) * jnp.stack(
        [powers[b][:, 0] * ((2.0 * narrow[:, b]) ** b)[:, None] for b in range(BASES)], axis=1
    )
    norm = 1.0 / jnp.sum(raw, axis=2)
    scalars = jnp.concatenate([narrow[:, :, None], norm[:, :, None], spatial_coef], axis=2)
    scalars = scalars.reshape(visits, BASES * SCALARS)
    f32, dma = jnp.float32, pltpu.SemaphoreType.DMA
    vmem = pl.BlockSpec(memory_space=pltpu.VMEM)
    return pl.pallas_call(
        functools.partial(kernel, tiles, owners),
        out_shape=jax.ShapeDtypeStruct((rows, cols), f32),
        in_specs=[pl.BlockSpec(memory_space=pltpu.SMEM), vmem, vmem, vmem],
        out_specs=vmem,
        scratch_shapes=[
            pltpu.VMEM((2, visits, HALO, cols), f32),
            pltpu.VMEM((owners, visits, share, BLOCK), f32),
            pltpu.VMEM((owners, visits, share, BLOCK), f32),
            pltpu.VMEM((owners, visits, share, BLOCK), f32),
            pltpu.VMEM((owners, visits, share, BLOCK), f32),
            pltpu.VMEM((BASES * rows, cols + 2 * SIDE), jnp.bfloat16),
            pltpu.VMEM((BASES * rows, cols + 2 * SIDE), jnp.bfloat16),
            pltpu.VMEM((owners * share, BLOCK), f32),
            pltpu.VMEM((owners, share, BLOCK), f32),
            dma((2, visits)),
            dma((2, visits)),
            dma((owners,)),
            dma((owners,)),
            dma((owners, visits)),
            dma((owners, visits)),
            dma((owners,)),
            dma((owners,)),
        ],
        compiler_params=pltpu.CompilerParams(
            collective_id=0, has_side_effects=True, vmem_limit_bytes=48 * 1024 * 1024
        ),
    )(scalars, exposure, variance, usable)


def solution(mesh):
    in_specs = (
        P("visit", ("patch", "tile"), None),
        P("visit", ("patch", "tile"), None),
        P("visit", ("patch", "tile"), None),
        P(("patch", "visit"), None),
        P(("patch", "visit"), None, None),
    )
    out_specs = P(("patch", "tile"), None)
    return jax.shard_map(
        per_device, mesh=mesh, in_specs=in_specs, out_specs=out_specs, check_vma=False
    )
```

```python
import functools

import jax
import jax.numpy as jnp
from jax import lax
from jax.experimental import pallas as pl
from jax.experimental.pallas import tpu as pltpu
from jax.sharding import PartitionSpec as P

KHALF = 15
BASES = 3
TERMS = 6
HALO = 16
BLOCK = 256
SIDE = 128
HALVES = 2
MESH = pl.DeviceIdType.MESH

big_value = 1e30


def band(offsets, narrow, norm, basis_id):
    square = (offsets * offsets).astype(jnp.float32)
    profile = jnp.exp(-square * narrow) * norm
    for _ in range(basis_id):
        profile = profile * (square * (2.0 * narrow))
    return jnp.where(jnp.abs(offsets) <= KHALF, profile, 0.0)


def split(values):
    high = values.astype(jnp.bfloat16)
    low = (values - high.astype(jnp.float32)).astype(jnp.bfloat16)
    return high, low


def dot(a, b):
    return jnp.dot(a, b, preferred_element_type=jnp.float32)


def kernel(
    tiles, owners,
    width_ref, coef_ref, expo_hbm, var_hbm, use_hbm, out_ref,
    expo_ref, var_ref, use_ref, halo, w_own, m_own, w_got, m_got, vert_hi, vert_lo, total, result,
    expo_sem, var_sem, use_sem, halo_send, halo_got, w_send, w_recv, m_send, m_recv, r_send, r_recv,
):
    visits, rows, cols = expo_ref.shape
    blocks = cols // BLOCK
    mine_blocks = blocks // owners
    share = mine_blocks * rows
    me = lax.axis_index("visit")
    tile = lax.axis_index("tile")
    has_up = tile > 0
    has_down = tile < tiles - 1
    far_first = sorted(range(1, owners), key=lambda d: (abs(2 * d - owners), d))
    peers = [lax.rem(me + d, owners) for d in far_first]
    load_var = pltpu.make_async_copy(var_hbm, var_ref, var_sem)
    load_use = pltpu.make_async_copy(use_hbm, use_ref, use_sem)
    load_expo = pltpu.make_async_copy(expo_hbm, expo_ref, expo_sem)
    load_var.start()
    load_use.start()
    load_expo.start()

    barrier = pltpu.get_barrier_semaphore()
    for peer in peers:
        pl.semaphore_signal(barrier, inc=1, device_id={"visit": peer}, device_id_type=MESH)

    @pl.when(has_up)
    def _():
        pl.semaphore_signal(barrier, inc=1, device_id={"tile": tile - 1}, device_id_type=MESH)

    @pl.when(has_down)
    def _():
        pl.semaphore_signal(barrier, inc=1, device_id={"tile": tile + 1}, device_id_type=MESH)

    beside = has_up.astype(jnp.int32) + has_down.astype(jnp.int32)
    pl.semaphore_wait(barrier, owners - 1 + beside)

    def halo_copy(side, v):
        start = rows - HALO if side == 0 else 0
        return pltpu.make_async_remote_copy(
            src_ref=expo_hbm.at[v, pl.ds(start, HALO), :],
            dst_ref=halo.at[side, v],
            send_sem=halo_send.at[side, v],
            recv_sem=halo_got.at[side, v],
            device_id={"tile": tile + 1 if side == 0 else tile - 1},
            device_id_type=MESH,
        )

    @pl.when(has_down)
    def _():
        for v in range(visits):
            halo_copy(0, v).start()

    @pl.when(has_up)
    def _():
        for v in range(visits):
            halo_copy(1, v).start()

    @pl.when(jnp.logical_not(has_up))
    def _():
        halo[0] = jnp.zeros(halo.shape[1:], jnp.float32)

    @pl.when(jnp.logical_not(has_down))
    def _():
        halo[1] = jnp.zeros(halo.shape[1:], jnp.float32)

    def w_copy(peer, k):
        return pltpu.make_async_remote_copy(
            src_ref=w_own.at[peer], dst_ref=w_got.at[me],
            send_sem=w_send.at[k], recv_sem=w_recv.at[me],
            device_id={"visit": peer}, device_id_type=MESH,
        )

    half = share // HALVES

    def m_copy(peer, k, v, h):
        return pltpu.make_async_remote_copy(
            src_ref=m_own.at[peer, v, pl.ds(h * half, half)], dst_ref=m_got.at[me, v, pl.ds(h * half, half)],
            send_sem=m_send.at[k, v, h], recv_sem=m_recv.at[me, v, h],
            device_id={"visit": peer}, device_id_type=MESH,
        )

    def r_copy(peer, k, h):
        return pltpu.make_async_remote_copy(
            src_ref=result.at[me, pl.ds(h * half, half)], dst_ref=result.at[me, pl.ds(h * half, half)],
            send_sem=r_send.at[k, h], recv_sem=r_recv.at[me, h],
            device_id={"visit": peer}, device_id_type=MESH,
        )

    def weights_for(owner):
        def step(v, carry):
            for j in range(mine_blocks):
                first = pl.multiple_of((owner * mine_blocks + j) * BLOCK, BLOCK)
                there = pl.ds(first, BLOCK)
                w_own[owner, v, pl.ds(j * rows, rows), :] = jnp.where(
                    use_ref[v, :, there] > 0, 1.0 / var_ref[v, :, there], 0.0
                )
            return carry

        lax.fori_loop(0, visits, step, 0)

    load_var.wait()
    load_use.wait()
    for k, peer in enumerate(peers):
        weights_for(peer)
        w_copy(peer, k).start()
    weights_for(me)
    load_expo.wait()

    wide = cols + 2 * SIDE
    for ref in (vert_hi, vert_lo):
        ref[:, pl.ds(0, SIDE)] = jnp.zeros((BASES * rows, SIDE), jnp.bfloat16)
        ref[:, pl.ds(wide - SIDE, SIDE)] = jnp.zeros((BASES * rows, SIDE), jnp.bfloat16)

    reach = rows + 2 * HALO
    depth = BLOCK + 2 * SIDE
    stacked = blocks * rows

    def visit_step(v, carry):
        @pl.when(has_up)
        def _():
            halo_copy(0, v).wait_recv()

        @pl.when(has_down)
        def _():
            halo_copy(1, v).wait_recv()

        lane = lax.broadcasted_iota(jnp.int32, (8, 2 * SIDE), 1)
        scales = []
        for b in range(BASES):
            width = jnp.full((1, 1), width_ref[v, b], jnp.float32)
            narrow = 0.5 / (width * width)
            whole = jnp.sum(band(lane - SIDE, narrow, 1.0, b), axis=1, keepdims=True)
            scales.append((narrow, 1.0 / whole[0:1]))

        out_row = lax.broadcasted_iota(jnp.int32, (rows, 3 * reach), 0)
        in_row = lax.broadcasted_iota(jnp.int32, (rows, 3 * reach), 1)
        third = in_row >= 2 * reach
        in_row = jnp.where(third, in_row - 2 * reach, jnp.where(in_row >= reach, in_row - reach, in_row))
        pieces = []
        for b in range(BASES):
            mat = band(in_row - HALO - out_row, *scales[b], b)
            high = mat.astype(jnp.bfloat16).astype(jnp.float32)
            pieces.append(jnp.where(third, mat - high, high))
        down = jnp.concatenate(pieces, axis=0).astype(jnp.bfloat16)

        def column_step(n, inner):
            there = pl.ds(pl.multiple_of(n * 2 * BLOCK, 2 * BLOCK), 2 * BLOCK)
            image = jnp.concatenate([halo[0, v, :, there], expo_ref[v, :, there], halo[1, v, :, there]], axis=0)
            high, low = split(image)
            vert = dot(down, jnp.concatenate([high, low, high], axis=0))
            high, low = split(vert)
            here = pl.ds(pl.multiple_of(n * 2 * BLOCK + SIDE, SIDE), 2 * BLOCK)
            vert_hi[:, here] = high
            vert_lo[:, here] = low
            return inner

        lax.fori_loop(0, blocks // 2, column_step, 0)

        in_col = lax.broadcasted_iota(jnp.int32, (depth, BLOCK), 0)
        out_col = lax.broadcasted_iota(jnp.int32, (depth, BLOCK), 1)
        for b in range(BASES):
            across_hi, across_lo = split(band(in_col - SIDE - out_col, *scales[b], b))
            c = [coef_ref[v, b, k] for k in range(TERMS)]
            for d in range(owners):
                left = [
                    jnp.concatenate(
                        [
                            ref[pl.ds(b * rows, rows), pl.ds((d * mine_blocks + j) * BLOCK, depth)]
                            for j in range(mine_blocks)
                        ],
                        axis=0,
                    )
                    for ref in (vert_hi, vert_lo)
                ]
                smooth = dot(left[0], across_hi) + dot(left[1], across_hi) + dot(left[0], across_lo)
                row = lax.broadcasted_iota(jnp.int32, (share, BLOCK), 0)
                col = lax.broadcasted_iota(jnp.int32, (share, BLOCK), 1)
                col = col + (d * mine_blocks + row // rows) * BLOCK
                row = row % rows + tile * rows
                y = row.astype(jnp.float32) * (2.0 / (tiles * rows - 1)) - 1.0
                x = col.astype(jnp.float32) * (2.0 / (cols - 1)) - 1.0
                factor = (c[0] + y * (c[2] + y * c[5])) + x * (c[1] + y * c[4] + x * c[3])
                term = factor * smooth
                here = pl.ds(d * share, share)
                if b == 0:
                    total[here, :] = term
                elif b < BASES - 1:
                    total[here, :] += term
                else:
                    m_own[d, v] = total[here, :] + term
        for h in range(HALVES):
            for k, peer in enumerate(peers):
                m_copy(peer, k, v, h).start()
        return carry

    lax.fori_loop(0, visits, visit_step, 0)

    def got_w(s):
        return pltpu.make_async_remote_copy(
            src_ref=w_own.at[s], dst_ref=w_got.at[s], send_sem=w_send.at[0], recv_sem=w_recv.at[s],
            device_id={"visit": s}, device_id_type=MESH,
        )

    def got_m(s, v, h):
        there = pl.ds(h * half, half)
        return pltpu.make_async_remote_copy(
            src_ref=m_own.at[s, v, there], dst_ref=m_got.at[s, v, there],
            send_sem=m_send.at[0, v, h], recv_sem=m_recv.at[s, v, h],
            device_id={"visit": s}, device_id_type=MESH,
        )

    def got_r(s, h):
        there = pl.ds(h * half, half)
        return pltpu.make_async_remote_copy(
            src_ref=result.at[s, there], dst_ref=result.at[s, there],
            send_sem=r_send.at[0, h], recv_sem=r_recv.at[s, h],
            device_id={"visit": s}, device_id_type=MESH,
        )

    for peer in peers:
        got_w(peer).wait_recv()

    sources = [(m_own, w_own, me)] + [(m_got, w_got, peer) for peer in peers]
    strip = 16

    def strip_step(i, carry):
        here = pl.ds(pl.multiple_of(i * strip, strip), strip)
        full = jnp.full((strip, BLOCK), big_value, jnp.float32)
        l1 = l2 = l3 = full
        h1 = h2 = h3 = -full
        for m_ref, w_ref, s in sources:
            for v in range(visits):
                m = m_ref[s, v, here, :]
                valid = w_ref[s, v, here, :] > 0.0
                low = jnp.where(valid, m, big_value)
                high = jnp.where(valid, m, -big_value)
                l3 = jnp.minimum(l3, jnp.maximum(l2, low))
                l2 = jnp.minimum(l2, jnp.maximum(l1, low))
                l1 = jnp.minimum(l1, low)
                h3 = jnp.maximum(h3, jnp.minimum(h2, high))
                h2 = jnp.maximum(h2, jnp.minimum(h1, high))
                h1 = jnp.maximum(h1, high)
        numer = jnp.zeros((strip, BLOCK), jnp.float32)
        denom = numer
        for m_ref, w_ref, s in sources:
            for v in range(visits):
                w = w_ref[s, v, here, :]
                m = jnp.minimum(jnp.maximum(m_ref[s, v, here, :], l3), h3)
                numer = numer + w * m
                denom = denom + w
        result[me, here, :] = numer / denom
        return carry

    for h in range(HALVES):
        for peer in peers:
            for v in range(visits):
                got_m(peer, v, h).wait_recv()
        lax.fori_loop(h * half // strip, (h + 1) * half // strip, strip_step, 0)
        for k, peer in enumerate(peers):
            r_copy(peer, k, h).start()
    for peer in peers:
        for h in range(HALVES):
            got_r(peer, h).wait_recv()
    for s in range(owners):
        for j in range(mine_blocks):
            out_ref[:, pl.ds((s * mine_blocks + j) * BLOCK, BLOCK)] = result[s, pl.ds(j * rows, rows), :]

    for k, peer in enumerate(peers):
        w_copy(peer, k).wait_send()
        for h in range(HALVES):
            for v in range(visits):
                m_copy(peer, k, v, h).wait_send()
            r_copy(peer, k, h).wait_send()

    @pl.when(has_down)
    def _():
        for v in range(visits):
            halo_copy(0, v).wait_send()

    @pl.when(has_up)
    def _():
        for v in range(visits):
            halo_copy(1, v).wait_send()


def per_device(exposure, variance, usable, basis_width, spatial_coef):
    visits, rows, cols = exposure.shape
    tiles, owners = lax.axis_size("tile"), lax.axis_size("visit")
    share = cols // BLOCK // owners * rows
    f32, dma = jnp.float32, pltpu.SemaphoreType.DMA
    vmem = pl.BlockSpec(memory_space=pltpu.VMEM)
    smem = pl.BlockSpec(memory_space=pltpu.SMEM)
    hbm = pl.BlockSpec(memory_space=pl.ANY)
    return pl.pallas_call(
        functools.partial(kernel, tiles, owners),
        out_shape=jax.ShapeDtypeStruct((rows, cols), f32),
        in_specs=[smem, smem, hbm, hbm, hbm],
        out_specs=vmem,
        scratch_shapes=[
            pltpu.VMEM((visits, rows, cols), f32),
            pltpu.VMEM((visits, rows, cols), f32),
            pltpu.VMEM((visits, rows, cols), jnp.int32),
            pltpu.VMEM((2, visits, HALO, cols), f32),
            pltpu.VMEM((owners, visits, share, BLOCK), f32),
            pltpu.VMEM((owners, visits, share, BLOCK), f32),
            pltpu.VMEM((owners, visits, share, BLOCK), f32),
            pltpu.VMEM((owners, visits, share, BLOCK), f32),
            pltpu.VMEM((BASES * rows, cols + 2 * SIDE), jnp.bfloat16),
            pltpu.VMEM((BASES * rows, cols + 2 * SIDE), jnp.bfloat16),
            pltpu.VMEM((owners * share, BLOCK), f32),
            pltpu.VMEM((owners, share, BLOCK), f32),
            dma(()),
            dma(()),
            dma(()),
            dma((2, visits)),
            dma((2, visits)),
            dma((owners,)),
            dma((owners,)),
            dma((owners, visits, HALVES)),
            dma((owners, visits, HALVES)),
            dma((owners, HALVES)),
            dma((owners, HALVES)),
        ],
        compiler_params=pltpu.CompilerParams(
            collective_id=0, has_side_effects=True, vmem_limit_bytes=56 * 1024 * 1024
        ),
    )(basis_width, spatial_coef, exposure, variance, usable)


def solution(mesh):
    in_specs = (
        P("visit", ("patch", "tile"), None),
        P("visit", ("patch", "tile"), None),
        P("visit", ("patch", "tile"), None),
        P(("patch", "visit"), None),
        P(("patch", "visit"), None, None),
    )
    out_specs = P(("patch", "tile"), None)
    return jax.shard_map(
        per_device, mesh=mesh, in_specs=in_specs, out_specs=out_specs, check_vma=False
    )
```

```python
import functools

import jax
import jax.numpy as jnp
from jax import lax
from jax.experimental import pallas as pl
from jax.experimental.pallas import tpu as pltpu
from jax.sharding import PartitionSpec as P

KHALF = 15
BASES = 3
TERMS = 6
HALO = 16
BLOCK = 256
SIDE = 128
HALVES = 4
MESH = pl.DeviceIdType.MESH

big_value = 1e30


def band(offsets, narrow, norm, basis_id):
    square = (offsets * offsets).astype(jnp.float32)
    profile = jnp.exp(-square * narrow) * norm
    for _ in range(basis_id):
        profile = profile * (square * (2.0 * narrow))
    return jnp.where(jnp.abs(offsets) <= KHALF, profile, 0.0)


def split(values):
    high = values.astype(jnp.bfloat16)
    low = (values - high.astype(jnp.float32)).astype(jnp.bfloat16)
    return high, low


def dot(a, b):
    return jnp.dot(a, b, preferred_element_type=jnp.float32)


def kernel(
    tiles, owners,
    width_ref, coef_ref, expo_hbm, var_hbm, use_hbm, out_ref,
    expo_ref, var_ref, use_ref, halo, w_own, m_own, w_got, m_got, vert_hi, vert_lo, total, result,
    expo_sem, var_sem, use_sem, halo_send, halo_got, w_send, w_recv, m_send, m_recv, r_send, r_recv,
):
    visits, rows, cols = expo_ref.shape
    blocks = cols // BLOCK
    mine_blocks = blocks // owners
    share = mine_blocks * rows
    me = lax.axis_index("visit")
    tile = lax.axis_index("tile")
    has_up = tile > 0
    has_down = tile < tiles - 1
    far_first = sorted(range(1, owners), key=lambda d: (abs(2 * d - owners), d))
    peers = [lax.rem(me + d, owners) for d in far_first]
    def loads(owner):
        width = mine_blocks * BLOCK
        there = pl.ds(pl.multiple_of(owner * width, BLOCK), width)
        return [
            pltpu.make_async_copy(hbm.at[:, :, there], ref.at[:, :, there], sem.at[owner])
            for hbm, ref, sem in ((var_hbm, var_ref, var_sem), (use_hbm, use_ref, use_sem))
        ]

    load_expo = pltpu.make_async_copy(expo_hbm, expo_ref, expo_sem)
    for owner in peers + [me]:
        for load in loads(owner):
            load.start()
    load_expo.start()

    barrier = pltpu.get_barrier_semaphore()
    for peer in peers:
        pl.semaphore_signal(barrier, inc=1, device_id={"visit": peer}, device_id_type=MESH)

    @pl.when(has_up)
    def _():
        pl.semaphore_signal(barrier, inc=1, device_id={"tile": tile - 1}, device_id_type=MESH)

    @pl.when(has_down)
    def _():
        pl.semaphore_signal(barrier, inc=1, device_id={"tile": tile + 1}, device_id_type=MESH)

    def weights_for(owner):
        for load in loads(owner):
            load.wait()

        def step(v, carry):
            for j in range(mine_blocks):
                first = pl.multiple_of((owner * mine_blocks + j) * BLOCK, BLOCK)
                there = pl.ds(first, BLOCK)
                w_own[owner, v, pl.ds(j * rows, rows), :] = jnp.where(
                    use_ref[v, :, there] > 0, 1.0 / var_ref[v, :, there], 0.0
                )
            return carry

        lax.fori_loop(0, visits, step, 0)

    weights_for(peers[0])
    beside = has_up.astype(jnp.int32) + has_down.astype(jnp.int32)
    pl.semaphore_wait(barrier, owners - 1 + beside)

    def halo_copy(side, v):
        start = rows - HALO if side == 0 else 0
        return pltpu.make_async_remote_copy(
            src_ref=expo_hbm.at[v, pl.ds(start, HALO), :],
            dst_ref=halo.at[side, v],
            send_sem=halo_send.at[side, v],
            recv_sem=halo_got.at[side, v],
            device_id={"tile": tile + 1 if side == 0 else tile - 1},
            device_id_type=MESH,
        )

    @pl.when(has_down)
    def _():
        for v in range(visits):
            halo_copy(0, v).start()

    @pl.when(has_up)
    def _():
        for v in range(visits):
            halo_copy(1, v).start()

    @pl.when(jnp.logical_not(has_up))
    def _():
        halo[0] = jnp.zeros(halo.shape[1:], jnp.float32)

    @pl.when(jnp.logical_not(has_down))
    def _():
        halo[1] = jnp.zeros(halo.shape[1:], jnp.float32)

    def w_copy(peer, k):
        return pltpu.make_async_remote_copy(
            src_ref=w_own.at[peer], dst_ref=w_got.at[me],
            send_sem=w_send.at[k], recv_sem=w_recv.at[me],
            device_id={"visit": peer}, device_id_type=MESH,
        )

    half = share // HALVES

    def m_copy(peer, k, v, h):
        return pltpu.make_async_remote_copy(
            src_ref=m_own.at[peer, v, pl.ds(h * half, half)], dst_ref=m_got.at[me, v, pl.ds(h * half, half)],
            send_sem=m_send.at[k, v, h], recv_sem=m_recv.at[me, v, h],
            device_id={"visit": peer}, device_id_type=MESH,
        )

    def r_copy(peer, k, h):
        return pltpu.make_async_remote_copy(
            src_ref=result.at[me, pl.ds(h * half, half)], dst_ref=result.at[me, pl.ds(h * half, half)],
            send_sem=r_send.at[k, h], recv_sem=r_recv.at[me, h],
            device_id={"visit": peer}, device_id_type=MESH,
        )

    for k, peer in enumerate(peers):
        if k > 0:
            weights_for(peer)
        w_copy(peer, k).start()
    weights_for(me)
    load_expo.wait()

    wide = cols + 2 * SIDE
    for ref in (vert_hi, vert_lo):
        ref[:, pl.ds(0, SIDE)] = jnp.zeros((BASES * rows, SIDE), jnp.bfloat16)
        ref[:, pl.ds(wide - SIDE, SIDE)] = jnp.zeros((BASES * rows, SIDE), jnp.bfloat16)

    reach = rows + 2 * HALO
    depth = BLOCK + 2 * SIDE
    stacked = blocks * rows

    def visit_step(v, carry):
        @pl.when(has_up)
        def _():
            halo_copy(0, v).wait_recv()

        @pl.when(has_down)
        def _():
            halo_copy(1, v).wait_recv()

        lane = lax.broadcasted_iota(jnp.int32, (8, 2 * SIDE), 1)
        scales = []
        for b in range(BASES):
            width = jnp.full((1, 1), width_ref[v, b], jnp.float32)
            narrow = 0.5 / (width * width)
            whole = jnp.sum(band(lane - SIDE, narrow, 1.0, b), axis=1, keepdims=True)
            scales.append((narrow, 1.0 / whole[0:1]))

        out_row = lax.broadcasted_iota(jnp.int32, (rows, 3 * reach), 0)
        in_row = lax.broadcasted_iota(jnp.int32, (rows, 3 * reach), 1)
        third = in_row >= 2 * reach
        in_row = jnp.where(third, in_row - 2 * reach, jnp.where(in_row >= reach, in_row - reach, in_row))
        pieces = []
        for b in range(BASES):
            mat = band(in_row - HALO - out_row, *scales[b], b)
            high = mat.astype(jnp.bfloat16).astype(jnp.float32)
            pieces.append(jnp.where(third, mat - high, high))
        down = jnp.concatenate(pieces, axis=0).astype(jnp.bfloat16)

        def column_step(n, inner):
            there = pl.ds(pl.multiple_of(n * 2 * BLOCK, 2 * BLOCK), 2 * BLOCK)
            image = jnp.concatenate([halo[0, v, :, there], expo_ref[v, :, there], halo[1, v, :, there]], axis=0)
            high, low = split(image)
            vert = dot(down, jnp.concatenate([high, low, high], axis=0))
            high, low = split(vert)
            here = pl.ds(pl.multiple_of(n * 2 * BLOCK + SIDE, SIDE), 2 * BLOCK)
            vert_hi[:, here] = high
            vert_lo[:, here] = low
            return inner

        lax.fori_loop(0, blocks // 2, column_step, 0)

        in_col = lax.broadcasted_iota(jnp.int32, (depth, BLOCK), 0)
        out_col = lax.broadcasted_iota(jnp.int32, (depth, BLOCK), 1)
        for b in range(BASES):
            across_hi, across_lo = split(band(in_col - SIDE - out_col, *scales[b], b))
            c = [coef_ref[v, b, k] for k in range(TERMS)]
            for d in range(owners):
                left = [
                    jnp.concatenate(
                        [
                            ref[pl.ds(b * rows, rows), pl.ds((d * mine_blocks + j) * BLOCK, depth)]
                            for j in range(mine_blocks)
                        ],
                        axis=0,
                    )
                    for ref in (vert_hi, vert_lo)
                ]
                smooth = dot(left[0], across_hi) + dot(left[1], across_hi) + dot(left[0], across_lo)
                row = lax.broadcasted_iota(jnp.int32, (share, BLOCK), 0)
                col = lax.broadcasted_iota(jnp.int32, (share, BLOCK), 1)
                col = col + (d * mine_blocks + row // rows) * BLOCK
                row = row % rows + tile * rows
                y = row.astype(jnp.float32) * (2.0 / (tiles * rows - 1)) - 1.0
                x = col.astype(jnp.float32) * (2.0 / (cols - 1)) - 1.0
                factor = (c[0] + y * (c[2] + y * c[5])) + x * (c[1] + y * c[4] + x * c[3])
                term = factor * smooth
                here = pl.ds(d * share, share)
                if b == 0:
                    total[here, :] = term
                elif b < BASES - 1:
                    total[here, :] += term
                else:
                    m_own[d, v] = total[here, :] + term
        for h in range(HALVES):
            for k, peer in enumerate(peers):
                m_copy(peer, k, v, h).start()
        return carry

    lax.fori_loop(0, visits, visit_step, 0)

    def got_w(s):
        return pltpu.make_async_remote_copy(
            src_ref=w_own.at[s], dst_ref=w_got.at[s], send_sem=w_send.at[0], recv_sem=w_recv.at[s],
            device_id={"visit": s}, device_id_type=MESH,
        )

    def got_m(s, v, h):
        there = pl.ds(h * half, half)
        return pltpu.make_async_remote_copy(
            src_ref=m_own.at[s, v, there], dst_ref=m_got.at[s, v, there],
            send_sem=m_send.at[0, v, h], recv_sem=m_recv.at[s, v, h],
            device_id={"visit": s}, device_id_type=MESH,
        )

    def got_r(s, h):
        there = pl.ds(h * half, half)
        return pltpu.make_async_remote_copy(
            src_ref=result.at[s, there], dst_ref=result.at[s, there],
            send_sem=r_send.at[0, h], recv_sem=r_recv.at[s, h],
            device_id={"visit": s}, device_id_type=MESH,
        )

    for peer in peers:
        got_w(peer).wait_recv()

    sources = [(m_own, w_own, me)] + [(m_got, w_got, peer) for peer in peers]
    strip = min(16, half)

    def strip_step(i, carry):
        here = pl.ds(pl.multiple_of(i * strip, strip), strip)
        full = jnp.full((strip, BLOCK), big_value, jnp.float32)
        l1 = l2 = l3 = full
        h1 = h2 = h3 = -full
        for m_ref, w_ref, s in sources:
            for v in range(visits):
                m = m_ref[s, v, here, :]
                valid = w_ref[s, v, here, :] > 0.0
                low = jnp.where(valid, m, big_value)
                high = jnp.where(valid, m, -big_value)
                l3 = jnp.minimum(l3, jnp.maximum(l2, low))
                l2 = jnp.minimum(l2, jnp.maximum(l1, low))
                l1 = jnp.minimum(l1, low)
                h3 = jnp.maximum(h3, jnp.minimum(h2, high))
                h2 = jnp.maximum(h2, jnp.minimum(h1, high))
                h1 = jnp.maximum(h1, high)
        numer = jnp.zeros((strip, BLOCK), jnp.float32)
        denom = numer
        for m_ref, w_ref, s in sources:
            for v in range(visits):
                w = w_ref[s, v, here, :]
                m = jnp.minimum(jnp.maximum(m_ref[s, v, here, :], l3), h3)
                numer = numer + w * m
                denom = denom + w
        result[me, here, :] = numer / denom
        return carry

    for h in range(HALVES):
        for peer in peers:
            for v in range(visits):
                got_m(peer, v, h).wait_recv()
        lax.fori_loop(h * half // strip, (h + 1) * half // strip, strip_step, 0)
        for k, peer in enumerate(peers):
            r_copy(peer, k, h).start()
    for peer in peers:
        for h in range(HALVES):
            got_r(peer, h).wait_recv()
    for s in range(owners):
        for j in range(mine_blocks):
            out_ref[:, pl.ds((s * mine_blocks + j) * BLOCK, BLOCK)] = result[s, pl.ds(j * rows, rows), :]

    for k, peer in enumerate(peers):
        w_copy(peer, k).wait_send()
        for h in range(HALVES):
            for v in range(visits):
                m_copy(peer, k, v, h).wait_send()
            r_copy(peer, k, h).wait_send()

    @pl.when(has_down)
    def _():
        for v in range(visits):
            halo_copy(0, v).wait_send()

    @pl.when(has_up)
    def _():
        for v in range(visits):
            halo_copy(1, v).wait_send()


def per_device(exposure, variance, usable, basis_width, spatial_coef):
    visits, rows, cols = exposure.shape
    tiles, owners = lax.axis_size("tile"), lax.axis_size("visit")
    share = cols // BLOCK // owners * rows
    f32, dma = jnp.float32, pltpu.SemaphoreType.DMA
    vmem = pl.BlockSpec(memory_space=pltpu.VMEM)
    smem = pl.BlockSpec(memory_space=pltpu.SMEM)
    hbm = pl.BlockSpec(memory_space=pl.ANY)
    return pl.pallas_call(
        functools.partial(kernel, tiles, owners),
        out_shape=jax.ShapeDtypeStruct((rows, cols), f32),
        in_specs=[smem, smem, hbm, hbm, hbm],
        out_specs=vmem,
        scratch_shapes=[
            pltpu.VMEM((visits, rows, cols), f32),
            pltpu.VMEM((visits, rows, cols), f32),
            pltpu.VMEM((visits, rows, cols), jnp.int32),
            pltpu.VMEM((2, visits, HALO, cols), f32),
            pltpu.VMEM((owners, visits, share, BLOCK), f32),
            pltpu.VMEM((owners, visits, share, BLOCK), f32),
            pltpu.VMEM((owners, visits, share, BLOCK), f32),
            pltpu.VMEM((owners, visits, share, BLOCK), f32),
            pltpu.VMEM((BASES * rows, cols + 2 * SIDE), jnp.bfloat16),
            pltpu.VMEM((BASES * rows, cols + 2 * SIDE), jnp.bfloat16),
            pltpu.VMEM((owners * share, BLOCK), f32),
            pltpu.VMEM((owners, share, BLOCK), f32),
            dma(()),
            dma((owners,)),
            dma((owners,)),
            dma((2, visits)),
            dma((2, visits)),
            dma((owners,)),
            dma((owners,)),
            dma((owners, visits, HALVES)),
            dma((owners, visits, HALVES)),
            dma((owners, HALVES)),
            dma((owners, HALVES)),
        ],
        compiler_params=pltpu.CompilerParams(
            collective_id=0, has_side_effects=True, vmem_limit_bytes=56 * 1024 * 1024
        ),
    )(basis_width, spatial_coef, exposure, variance, usable)


def solution(mesh):
    in_specs = (
        P("visit", ("patch", "tile"), None),
        P("visit", ("patch", "tile"), None),
        P("visit", ("patch", "tile"), None),
        P(("patch", "visit"), None),
        P(("patch", "visit"), None, None),
    )
    out_specs = P(("patch", "tile"), None)
    return jax.shard_map(
        per_device, mesh=mesh, in_specs=in_specs, out_specs=out_specs, check_vma=False
    )
```
